32 devices in a mesh: chan: 8 (over z, core), rec: 4 (over y, x).
Axes of the slice: x: 2, y: 2, z: 4, core: 2. Of those that a mesh axis runs over, the one named last changes fastest.
Arguments:
- strain_rate: bfloat16 [16, 4096, 2048], P('rec', 'chan'), may hold values from -6 to 6
Outputs:
- stacked_cross: float32 [4096, 8192], P(('chan', 'rec'))
The draws below stay inside these ranges and needn't reach their ends.
All inputs are finite; a program needn't handle non-finite values.
Results may differ from the reference program's by a relative error of at most 0.003.
Values sent between devices are 32-bit elements; how exact they have to be, the bound alone decides.
No kernel may reach another device: no remote copies, remote signals or barrier semaphores. Data moves between devices by JAX's collectives and lax.ppermute only.
A program may use at most 128 MiB of HBM per device.

```python
import math
import jax
import jax.numpy as jnp
from jax import lax

S = 2048
F = 64
K = 64
BIN0 = 32
CHANNELS = 4096
RECORDS = 16


def shard_levels(stream_key, shape, pieces, least, high):
    gain, own = 1.0, jax.random.fold_in(stream_key, 6)
    for position, parts in pieces:
        draws = jnp.exp(jax.random.uniform(jax.random.fold_in(own, position), (parts,), jnp.float32, least / len(pieces), high / len(pieces)))
        gain = gain * jnp.repeat(draws, shape[position] // parts).reshape([-1 if axis == position else 1 for axis in range(len(shape))])
    return gain


def gaussian(stream_key, dims, spread, most, split=(), kind=jnp.bfloat16):
    values = jax.random.normal(stream_key, dims, jnp.float32) * spread
    if len(split) > 0:
        values = shard_levels(stream_key, dims, split, -0.22, 0.18) * values
    return jnp.clip(values, min=-most, max=most).astype(kind)


def setup_inputs(seed: int = 0) -> dict:
    key_of = jax.random.split(jax.random.key(seed), 2)
    strain_rate = gaussian(key_of[0], (RECORDS, CHANNELS, S), 1.0, 6.0, ((0, 4), (1, 8)))
    return dict(strain_rate=strain_rate)


def make_tables():
    sample_idx = jnp.arange(S, dtype=jnp.int32)
    bin_idx = BIN0 + jnp.arange(F, dtype=jnp.int32)
    phase = sample_idx[:, None] * bin_idx[None, :] % S
    angle = 2.0 * math.pi / S * phase.astype(jnp.float32)
    return (jnp.cos(angle).astype(jnp.bfloat16), jnp.sin(angle).astype(jnp.bfloat16))

def whiten(block, cos_table, sin_table):
    spec_re = jnp.dot(block, cos_table, preferred_element_type=jnp.float32)
    spec_im = -jnp.dot(block, sin_table, preferred_element_type=jnp.float32)
    power = lax.optimization_barrier(jnp.mean(spec_re * spec_re + spec_im * spec_im, axis=-1, keepdims=True))
    scale = 1.0 / jnp.sqrt(power + 1e-06)
    return jnp.concatenate([spec_re * scale, spec_im * scale], axis=-1)

def cross_block(own_rows, ext_rows):
    count = own_rows.shape[0]
    offsets = jnp.arange(K, dtype=jnp.int32)
    part = jax.vmap(lambda k: lax.dynamic_slice_in_dim(ext_rows, k, count, 0))(offsets)
    a_re = own_rows[None, :, :F]
    a_im = own_rows[None, :, F:]
    b_re = part[:, :, :F]
    b_im = part[:, :, F:]
    cross_re = a_re * b_re + a_im * b_im
    cross_im = a_im * b_re - a_re * b_im
    return jnp.transpose(jnp.concatenate([cross_re, cross_im], axis=-1), (1, 0, 2))

def reference(strain_rate):
    cos_table, sin_table = make_tables()
    whitened = lax.map(lambda rec: whiten(rec, cos_table, sin_table), strain_rate)
    extended = jnp.pad(whitened, ((0, 0), (0, K - 1), (0, 0)))

    def add_record(total, pair):
        return (total + cross_block(pair[0], pair[1]), None)
    start = jnp.zeros((CHANNELS, K, 2 * F), jnp.float32)
    total, _ = lax.scan(add_record, start, (whitened, extended))
    return (total / RECORDS).reshape(CHANNELS, K * 2 * F)
```

```python
import functools
import math

import jax
import jax.numpy as jnp
import numpy as np
from jax import lax
from jax.experimental import pallas as pl
from jax.experimental.pallas import tpu as pltpu
from jax.sharding import PartitionSpec as P

S = 2048
F = 64
K = 64
BIN0 = 32
W = 2 * F
SUB = 8


def make_table():
    phase = np.arange(S)[:, None] * (BIN0 + np.arange(F))[None, :] % S
    angle = 2.0 * math.pi / S * phase
    return np.concatenate([np.cos(angle), -np.sin(angle)], axis=1).astype(jnp.bfloat16)


def whiten_kernel(pos_ref, table_ref, *refs):
    count = len(refs) // 2
    for strain_ref, out_ref in zip(refs[:count], refs[count:]):
        spec = jnp.dot(strain_ref[0], table_ref[...], preferred_element_type=jnp.float32)
        power = jnp.sum(spec * spec, axis=-1, keepdims=True) * (1.0 / F)
        out_ref[0] = spec * lax.rsqrt(power + 1e-06)


def whiten(strain, table, pos, pick, rows):
    records, _, samples = strain.shape

    def in_spec(i):
        return pl.BlockSpec((1, rows, samples), lambda r, p: (r, p[i], 0))

    out = jax.ShapeDtypeStruct((records, rows, W), jnp.float32)
    return pl.pallas_call(
        whiten_kernel,
        out_shape=[out] * len(pick),
        grid_spec=pltpu.PrefetchScalarGridSpec(
            num_scalar_prefetch=1,
            grid=(records,),
            in_specs=[pl.BlockSpec((samples, W), lambda r, p: (0, 0))] + [in_spec(i) for i in pick],
            out_specs=[pl.BlockSpec((1, rows, W), lambda r, p: (r, 0, 0))] * len(pick),
        ),
        compiler_params=pltpu.CompilerParams(vmem_limit_bytes=24 * 2**20),
        cost_estimate=pl.CostEstimate(
            flops=2 * records * rows * samples * W * len(pick),
            bytes_accessed=2 * records * rows * samples * len(pick),
            transcendentals=0,
        ),
        name="whiten",
    )(pos, table, *([strain] * len(pick)))


def cross_kernel(scale, groups, k_range, has_acc, refs_per_group, *refs):
    refs = list(refs)
    acc_ref = refs.pop(0) if has_acc else None
    ins = [[refs.pop(0) for _ in range(n)] for n in refs_per_group]
    out_ref, a_ref, b_ref = refs
    t = pl.program_id(0)

    @pl.when(t == 0)
    def _():
        lane = lax.broadcasted_iota(jnp.int32, (1, W), 1)
        low = lane < F
        g = 0
        for parts in ins:
            n = parts[0].shape[0]
            for r in range(n):
                at = 0
                for i, part in enumerate(parts):
                    rows = part.shape[1]
                    w = part[r]
                    turned = pltpu.roll(w, F, 1)
                    b_ref[0, g, at : at + rows] = jnp.where(low, w, turned)
                    b_ref[1, g, at : at + rows] = jnp.where(low, turned, w)
                    if i == 0:
                        own = a_ref.shape[2]
                        a_ref[0, g] = w[:own] * scale
                        a_ref[1, g] = (jnp.where(low, turned, -turned))[:own] * scale
                    at += rows
                g += 1

    first, last, tile = k_range(t)
    row0 = tile * SUB
    left = [
        (a_ref[0, g, pl.ds(row0, SUB)], a_ref[1, g, pl.ds(row0, SUB)]) for g in range(groups)
    ]

    def step(q, carry):
        for u in range(SUB):
            k = q * SUB + u
            total = acc_ref[:, pl.ds(k * W, W)] if has_acc else None
            for g in range(groups):
                term = left[g][0] * b_ref[0, g, pl.ds(row0 + k, SUB)]
                total = term if total is None else total + term
                total = total + left[g][1] * b_ref[1, g, pl.ds(row0 + k, SUB)]
            out_ref[:, pl.ds(k * W, W)] = total
        return carry

    lax.fori_loop(first, last, step, 0)


def cross(groups_in, rows, scale, acc=None, region="all"):
    tiles = rows // SUB
    steps = K // SUB
    tile0 = 0
    if region == "all":
        k_range = lambda t: (0, steps, t)
    elif region == "main":
        k_range = lambda t: (0, jnp.minimum(steps, tiles - 1 - t), t)
    else:
        tile0 = tiles - steps
        tiles = steps
        k_range = lambda t: (steps - 1 - t, steps, t + tile0)
    records = sum(g[0].shape[0] for g in groups_in)
    ext = max(sum(p.shape[1] for p in g) for g in groups_in)
    flat = [p for g in groups_in for p in g]
    whole = [pl.BlockSpec(p.shape, lambda t: (0, 0, 0)) for p in flat]
    block = pl.BlockSpec((SUB, K * W), lambda t: (t + tile0, 0))
    return pl.pallas_call(
        functools.partial(
            cross_kernel, scale, records, k_range, acc is not None, [len(g) for g in groups_in]
        ),
        out_shape=jax.ShapeDtypeStruct((rows, K * W), jnp.float32),
        grid=(tiles,),
        in_specs=([block] if acc is not None else []) + whole,
        out_specs=block,
        scratch_shapes=[
            pltpu.VMEM((2, records, rows, W), jnp.float32),
            pltpu.VMEM((2, records, ext, W), jnp.float32),
        ],
        input_output_aliases={0: 0} if acc is not None else {},
        compiler_params=pltpu.CompilerParams(vmem_limit_bytes=32 * 2**20),
        cost_estimate=pl.CostEstimate(
            flops=8 * records * rows * K * W, bytes_accessed=4 * rows * K * W, transcendentals=0
        ),
        name="cross_" + region,
    )(*([acc] if acc is not None else []), *flat)


def xor_pairs(size, by):
    return [(i, i ^ by) for i in range(size)]


def shifted(shard, axis, by):
    length = lax.axis_size(axis)
    pairs = [(i, i + by) for i in range(length) if 0 <= i + by < length]
    return lax.ppermute(shard, axis, pairs)


def per_device(strain):
    table = jnp.asarray(make_table())
    records, channels, _ = strain.shape
    size = lax.axis_size("rec")
    rows = channels // size
    scale = 1.0 / (records * size)
    zero = jnp.zeros((1,), jnp.int32)
    me = lax.axis_index("rec")

    (spectra,) = whiten(strain, table, zero, [0], channels)
    below = shifted(spectra[:, :K], "chan", -1)
    extended = jnp.concatenate([spectra, below], axis=1)
    pieces = []
    for by in range(size):
        part = lax.dynamic_slice_in_dim(extended, (me ^ by) * rows, rows + K, 1)
        pieces.append(lax.ppermute(part, "rec", xor_pairs(size, by)) if by else part)
    return cross([[p] for p in pieces], rows, scale)


def solution(mesh):
    placed = (P("rec", "chan", None),)
    return jax.shard_map(
        per_device, mesh=mesh, in_specs=placed, out_specs=P(("chan", "rec"), None), check_vma=False
    )
```

```python
import functools
import math

import jax
import jax.numpy as jnp
from jax import lax
from jax.experimental import pallas as pl
from jax.experimental.pallas import tpu as pltpu
from jax.sharding import PartitionSpec as P

S = 2048
F = 64
K = 64
BIN0 = 32
W = 2 * F
SUB = 8
TILES = 4
SPAN = SUB * TILES
STEPS = K // SUB
HALF = SUB // 2
MOST = 8
VMEM = pl.BlockSpec(memory_space=pltpu.VMEM)
HBM = pl.BlockSpec(memory_space=pltpu.HBM)


def fill_table(table_ref):
    fine = 64

    def angle(rows, every, turn):
        n = lax.broadcasted_iota(jnp.int32, (rows, W), 0) * every
        lane = lax.broadcasted_iota(jnp.int32, (rows, W), 1)
        phase = n * (BIN0 + lax.rem(lane, F)) + jnp.where(lane < F, 0, S // 4) * (every == 1) + turn
        return jnp.cos(lax.rem(phase, S).astype(jnp.float32) * (2.0 * math.pi / S))

    cos_a, sin_a = angle(S // fine, fine, 0), angle(S // fine, fine, 3 * S // 4)
    cos_b, sin_b = angle(fine, 1, 0), angle(fine, 1, 3 * S // 4)
    for i in range(S // fine):
        rows = cos_a[i : i + 1] * cos_b - sin_a[i : i + 1] * sin_b
        table_ref[fine * i : fine * (i + 1)] = rows.astype(jnp.bfloat16)


def whiten_kernel(jobs, pair, has_table, strain_hbm, *refs):
    refs = list(refs)
    table_ref = refs.pop(0) if has_table else None
    outs = [refs.pop(0) for _ in jobs]
    made_ref = None if has_table else refs.pop(0)
    sems, bufs = refs[0], refs[1:]
    me = lax.axis_index("rec")
    copies = []
    for (start, rows), buf in zip(jobs, bufs):
        at = pl.multiple_of(start(me), rows)
        for r in range(0, buf.shape[0], pair):
            copy = pltpu.make_async_copy(
                strain_hbm.at[pl.ds(r, pair), pl.ds(at, rows), :],
                buf.at[pl.ds(r, pair)],
                sems.at[len(copies)],
            )
            copy.start()
            copies.append(copy)
    if not has_table:
        fill_table(made_ref)
        table_ref = made_ref
    at = 0
    for (_, rows), buf, out in zip(jobs, bufs, outs):
        for r in range(0, buf.shape[0], pair):
            copies[at].wait()
            at += 1
            block = buf[r : r + pair].reshape(pair * rows, S)
            spec = jnp.dot(block, table_ref[...], preferred_element_type=jnp.float32)
            power = jnp.sum(spec * spec, axis=-1, keepdims=True) * (1.0 / F)
            out[r : r + pair] = (spec * lax.rsqrt(power + 1e-06)).reshape(pair, rows, W)


def whiten(strain, jobs, pair, table=None):
    records = strain.shape[0]
    total = sum(rows for _, rows in jobs)
    outs = [jax.ShapeDtypeStruct((records, rows, W), jnp.float32) for _, rows in jobs]
    if table is None:
        outs.append(jax.ShapeDtypeStruct((S, W), jnp.bfloat16))
    return pl.pallas_call(
        functools.partial(whiten_kernel, jobs, pair, table is not None),
        out_shape=outs,
        in_specs=[HBM] + ([] if table is None else [VMEM]),
        out_specs=[VMEM] * len(outs),
        scratch_shapes=[pltpu.SemaphoreType.DMA((len(jobs) * (records // pair),))]
        + [pltpu.VMEM((records, rows, S), jnp.bfloat16) for _, rows in jobs],
        compiler_params=pltpu.CompilerParams(vmem_limit_bytes=50 * 2**20),
        cost_estimate=pl.CostEstimate(
            flops=2 * records * total * S * W,
            bytes_accessed=2 * records * total * S,
            transcendentals=0,
        ),
        name="whiten",
    )(strain, *([] if table is None else [table]))


def halo_kernel(size, own_ref, *refs):
    mains, below_ref, outs = refs[: size - 1], refs[size - 1], refs[size:]
    me = lax.axis_index("rec")
    blocks = [own_ref] + list(mains)
    for by in range(size):
        target = lax.bitwise_xor(me, by)
        out = outs[by]
        at = out.shape[1] - K
        if at:
            out[:, :at] = blocks[by][:, :at]
        for other in range(size):
            if other != by:

                @pl.when((target < size - 1) & (lax.bitwise_xor(me, other) == target + 1))
                def _():
                    out[:, at:] = blocks[other][:, :K]

        @pl.when(target == size - 1)
        def _():
            out[:, at:] = below_ref[...]


def prepare(scale, parts, g, r, a_ref, b_ref):
    low = lax.broadcasted_iota(jnp.int32, (1, W), 1) < F
    rows = a_ref.shape[2]
    at = 0
    for part in parts:
        w = part[r]
        turned = pltpu.roll(w, F, 1)
        b_ref[0, g, at : at + w.shape[0]] = jnp.where(low, turned - w, -(w + turned))
        b_ref[1, g, at : at + w.shape[0]] = jnp.where(low, w, turned)
        if at < rows:
            own, both = turned * scale, (w + turned) * scale
            n = min(rows - at, w.shape[0])
            a_ref[0, g, at : at + n] = own[:n]
            a_ref[1, g, at : at + n] = both[:n]
        at += w.shape[0]


def pack(g, b_ref):
    low = lax.broadcasted_iota(jnp.int32, (1, W), 1) < F
    ext = b_ref.shape[2] - SUB
    here = b_ref[1, g, 0:ext]
    there = b_ref[1, g, HALF : HALF + ext]
    b_ref[1, g, 0:ext] = jnp.where(low, here, there)


def step(q, tiles, row0, records, a_ref, b_ref, acc_ref, out_ref):
    low = lax.broadcasted_iota(jnp.int32, (SUB, W), 1) < F

    def add(total, term):
        return term if total is None else total + term

    for u in range(HALF):
        s = row0 + SUB * q + u
        places, sums = [], []
        for i in tiles:
            rows = pl.ds(pl.multiple_of(row0 + SUB * i, SUB), SUB)
            k = SUB * (q - i) + u
            cols = [pl.ds(pl.multiple_of(n * W, W), W) for n in (k, k + HALF)]
            places.append([(rows, col) for col in cols])
            sums.append([None] + [None if acc_ref is None else acc_ref[at] for at in places[-1]])
        for g in records:
            both = b_ref[1, g, pl.ds(s, SUB)]
            first = b_ref[0, g, pl.ds(s, SUB)]
            second = b_ref[0, g, pl.ds(s + HALF, SUB)]
            for x, i in enumerate(tiles):
                own = a_ref[0, g, pl.ds(row0 + SUB * i, SUB)]
                whole = a_ref[1, g, pl.ds(row0 + SUB * i, SUB)]
                p, t1, t2 = sums[x]
                sums[x] = [add(p, whole * both), add(t1, own * first), add(t2, own * second)]
        for (here, there), (p, t1, t2) in zip(places, sums):
            turned = pltpu.roll(p, F, 1)
            out_ref[here] = t1 + jnp.where(low, p, turned)
            out_ref[there] = t2 + jnp.where(low, turned, p)


def sweep(records, region, rows, a_ref, b_ref, acc_ref, out_ref):
    spans = rows // SPAN
    last = STEPS + TILES - 1
    bound = rows // SUB - 1
    args = (records, a_ref, b_ref, acc_ref, out_ref)

    def run(q, tiles, row0):
        step(q, tiles, row0, *args)

    def span(c, carry):
        row0 = pl.multiple_of(c * SPAN, SPAN)
        edge = bound - TILES * c
        lo, hi = TILES - 1, STEPS
        if region == "main":
            hi = jnp.clip(edge, TILES - 1, STEPS)
        if region == "halo":
            lo = jnp.clip(edge, TILES - 1, STEPS)
        if region != "halo":
            for q in range(TILES - 1):
                run(q, list(range(q + 1)), row0)
        lax.fori_loop(lo, hi, lambda q, n: (run(q, list(range(TILES)), row0), n)[1], 0)

        def tail():
            for q in range(STEPS, last):
                run(q, list(range(q - STEPS + 1, TILES)), row0)

        if region == "main":
            pl.when(edge >= last)(tail)
        else:
            tail()
        return carry

    first = spans - STEPS // TILES if region == "halo" else 0
    lax.fori_loop(first, spans, span, 0)


def cross_kernel(scale, counts, passes, has_acc, rows, *refs):
    refs = list(refs)
    acc_ref = refs.pop(0) if has_acc else None
    groups = [[refs.pop(0) for _ in range(n)] for n in counts]
    out_ref, a_ref, b_ref = refs
    g = 0
    for parts in groups:
        for r in range(parts[0].shape[0]):
            prepare(scale, parts, g, r, a_ref, b_ref)
            pack(g, b_ref)
            g += 1
    for records, region in passes:
        sweep(records, region, rows, a_ref, b_ref, acc_ref, out_ref)


def finish_kernel(scale, records, rows, acc_ref, main_ref, halo_ref, out_hbm, tail_ref, a_ref, b_ref, sems):
    half = rows - K
    top = pltpu.make_async_copy(acc_ref.at[pl.ds(0, half)], out_hbm.at[pl.ds(0, half)], sems.at[0])
    top.start()
    copies = [top]
    tiles = K // SUB

    def slab(i, lo, hi, source, shift):
        return pltpu.make_async_copy(
            source.at[pl.ds(half + SUB * i - shift, SUB), pl.ds(lo * W, (hi - lo) * W)],
            out_hbm.at[pl.ds(half + SUB * i, SUB), pl.ds(lo * W, (hi - lo) * W)],
            sems.at[len(copies)],
        )

    for i in range(tiles - 1):
        copy = slab(i, 0, K - SUB * (i + 1), acc_ref, 0)
        copy.start()
        copies.append(copy)
    for r in range(records):
        prepare(scale, [main_ref, halo_ref], r, r, a_ref, b_ref)
        pack(r, b_ref)
    sweep(range(records), "halo", rows, a_ref, b_ref, acc_ref, tail_ref)
    for i in range(tiles):
        copy = slab(i, K - SUB * (i + 1), K, tail_ref, 0)
        copy.start()
        copies.append(copy)
    for copy in copies:
        copy.wait()


def cost(records, rows):
    return pl.CostEstimate(flops=500 * records * rows * K * W, bytes_accessed=0, transcendentals=0)


def factors(records, rows):
    return [
        pltpu.VMEM((2, records, rows, W), jnp.float32),
        pltpu.VMEM((2, records, rows + K + SUB, W), jnp.float32),
    ]


def cross(groups, passes, rows, scale, acc=None):
    records = sum(g[0].shape[0] for g in groups)
    flat = [p for g in groups for p in g]
    return pl.pallas_call(
        functools.partial(
            cross_kernel, scale, [len(g) for g in groups], passes, acc is not None, rows
        ),
        out_shape=jax.ShapeDtypeStruct((rows, K * W), jnp.float32),
        in_specs=[VMEM] * (len(flat) + (acc is not None)),
        out_specs=VMEM,
        scratch_shapes=factors(records, rows),
        input_output_aliases={0: 0} if acc is not None else {},
        compiler_params=pltpu.CompilerParams(vmem_limit_bytes=28 * 2**20),
        cost_estimate=cost(records, rows),
        name="cross",
    )(*([acc] if acc is not None else []), *flat)


def finish(acc, main, halo, scale):
    records, rows, _ = main.shape
    return pl.pallas_call(
        functools.partial(finish_kernel, scale, records, rows),
        out_shape=jax.ShapeDtypeStruct((rows, K * W), jnp.float32),
        in_specs=[VMEM] * 3,
        out_specs=HBM,
        scratch_shapes=[pltpu.VMEM((rows, K * W), jnp.float32)]
        + factors(records, rows)
        + [pltpu.SemaphoreType.DMA((2 * K // SUB,))],
        compiler_params=pltpu.CompilerParams(vmem_limit_bytes=28 * 2**20),
        cost_estimate=cost(records, rows),
        name="finish",
    )(acc, main, halo)


def send(shard, by):
    size = lax.axis_size("rec")
    return lax.ppermute(shard, "rec", [(i, i ^ by) for i in range(size)])


def shifted(shard, axis, by):
    length = lax.axis_size(axis)
    pairs = [(i, i + by) for i in range(length) if 0 <= i + by < length]
    return lax.ppermute(shard, axis, pairs)


def per_device(strain):
    records, channels, _ = strain.shape
    size = lax.axis_size("rec")
    rows = channels // size
    scale = 1.0 / (records * size)
    if size == 4 and rows == 2 * K and records <= HALF:
        return four(strain, rows, scale)
    return general(strain, rows, scale)


def four(strain, rows, scale):
    records = strain.shape[0]
    pair = 2 if records % 2 == 0 else 1

    def block(by):
        return (lambda me: lax.bitwise_xor(me, by) * rows, rows)

    far, head, table = whiten(strain, [block(3), (lambda me: 0, K)], pair)
    far_in = send(far, 3)
    below = shifted(head, "chan", -1)
    one, two, own = whiten(strain, [block(1), block(2), block(0)], pair, table)
    full = jax.ShapeDtypeStruct((records, rows + K, W), jnp.float32)
    short = jax.ShapeDtypeStruct((records, K, W), jnp.float32)
    own_halo, one, two, far_halo = pl.pallas_call(
        functools.partial(halo_kernel, 4),
        out_shape=[short, full, full, short],
        in_specs=[VMEM] * 5,
        out_specs=[VMEM] * 4,
        compiler_params=pltpu.CompilerParams(vmem_limit_bytes=16 * 2**20),
        name="halo",
    )(own, one, two, far, below)
    one_in = send(one, 1)
    two_in = send(two, 2)
    far_halo_in = send(far_halo, 3)
    near = range(records)
    pairs = range(2 * records)
    acc = cross([[own, own_halo], [far_in]], [(pairs, "main"), (near, "halo")], rows, scale)
    acc = cross([[one_in], [two_in]], [(pairs, "all")], rows, scale, acc)
    return finish(acc, far_in, far_halo_in, scale)


def general(strain, rows, scale):
    records, channels, _ = strain.shape
    size = lax.axis_size("rec")
    me = lax.axis_index("rec")
    spectra, _ = whiten(strain, [(lambda me: 0, channels)], 1)
    below = shifted(spectra[:, :K], "chan", -1)
    extended = jnp.concatenate([spectra, below], axis=1)
    acc = None
    for by in range(size):
        to = lax.rem(me + by, size)
        part = lax.dynamic_slice_in_dim(extended, to * rows, rows + K, 1)
        if by:
            part = lax.ppermute(part, "rec", [(i, (i + by) % size) for i in range(size)])
        for r in range(0, records, MOST):
            some = part[r : r + MOST]
            acc = cross([[some]], [(range(some.shape[0]), "all")], rows, scale, acc)
    return acc


def solution(mesh):
    placed = (P("rec", "chan", None),)
    return jax.shard_map(
        per_device, mesh=mesh, in_specs=placed, out_specs=P(("chan", "rec"), None), check_vma=False
    )
```

```python
import functools
import math

import jax
import jax.numpy as jnp
from jax import lax
from jax.experimental import pallas as pl
from jax.experimental.pallas import tpu as pltpu
from jax.sharding import PartitionSpec as P

S = 2048
F = 64
K = 64
BIN0 = 32
W = 2 * F
SUB = 8
STEPS = K // SUB
HALF = SUB // 2
MOST = 8
VMEM = pl.BlockSpec(memory_space=pltpu.VMEM)
HBM = pl.BlockSpec(memory_space=pltpu.HBM)


def fill_table(table_ref):
    fine = 64

    def angle(rows, every, turn):
        n = lax.broadcasted_iota(jnp.int32, (rows, W), 0) * every
        lane = lax.broadcasted_iota(jnp.int32, (rows, W), 1)
        phase = n * (BIN0 + lax.rem(lane, F)) + jnp.where(lane < F, 0, S // 4) * (every == 1) + turn
        return jnp.cos(lax.rem(phase, S).astype(jnp.float32) * (2.0 * math.pi / S))

    cos_a, sin_a = angle(S // fine, fine, 0), angle(S // fine, fine, 3 * S // 4)
    cos_b, sin_b = angle(fine, 1, 0), angle(fine, 1, 3 * S // 4)
    for i in range(S // fine):
        rows = cos_a[i : i + 1] * cos_b - sin_a[i : i + 1] * sin_b
        table_ref[fine * i : fine * (i + 1)] = rows.astype(jnp.bfloat16)


def whiten_kernel(jobs, pair, strain_hbm, *refs):
    outs, head_ref, refs = refs[: len(jobs)], refs[len(jobs)], refs[len(jobs) + 1 :]
    table_ref, sems, bufs = refs[0], refs[1], refs[2:]
    me = lax.axis_index("rec")
    copies = []
    for (start, rows), buf in zip(jobs, bufs):
        at = pl.multiple_of(start(me), rows)
        for r in range(0, buf.shape[0], pair):
            copy = pltpu.make_async_copy(
                strain_hbm.at[pl.ds(r, pair), pl.ds(at, rows), :],
                buf.at[pl.ds(r, pair)],
                sems.at[len(copies)],
            )
            copy.start()
            copies.append(copy)
    fill_table(table_ref)
    at = 0
    for (start, rows), buf, out in zip(jobs, bufs, outs):
        for r in range(0, buf.shape[0], pair):
            copies[at].wait()
            at += 1
            block = buf[r : r + pair].reshape(pair * rows, S)
            spec = jnp.dot(block, table_ref[...], preferred_element_type=jnp.float32)
            power = jnp.sum(spec * spec, axis=-1, keepdims=True) * (1.0 / F)
            out[r : r + pair] = (spec * lax.rsqrt(power + 1e-06)).reshape(pair, rows, W)

        @pl.when(start(me) == 0)
        def _():
            head_ref[...] = out[:, :K]


def whiten(strain, jobs, pair):
    records = strain.shape[0]
    total = sum(rows for _, rows in jobs)
    outs = [jax.ShapeDtypeStruct((records, rows, W), jnp.float32) for _, rows in jobs]
    outs.append(jax.ShapeDtypeStruct((records, K, W), jnp.float32))
    return pl.pallas_call(
        functools.partial(whiten_kernel, jobs, pair),
        out_shape=outs,
        in_specs=[HBM],
        out_specs=[VMEM] * len(outs),
        scratch_shapes=[
            pltpu.VMEM((S, W), jnp.bfloat16),
            pltpu.SemaphoreType.DMA((len(jobs) * (records // pair),)),
        ]
        + [pltpu.VMEM((records, rows, S), jnp.bfloat16) for _, rows in jobs],
        compiler_params=pltpu.CompilerParams(vmem_limit_bytes=50 * 2**20),
        cost_estimate=pl.CostEstimate(
            flops=2 * records * total * S * W,
            bytes_accessed=2 * records * total * S,
            transcendentals=0,
        ),
        name="whiten",
    )(strain)


def halo_kernel(size, *refs):
    blocks, below_ref, outs = refs[:size], refs[size], refs[size + 1 :]
    me = lax.axis_index("rec")
    for by, out in enumerate(outs):
        target = lax.bitwise_xor(me, by)
        for other in range(size):
            if other != by:

                @pl.when((target < size - 1) & (lax.bitwise_xor(me, other) == target + 1))
                def _():
                    out[...] = blocks[other][:, :K]

        @pl.when(target == size - 1)
        def _():
            out[...] = below_ref[...]


def halos(blocks, below):
    size = len(blocks)
    return pl.pallas_call(
        functools.partial(halo_kernel, size),
        out_shape=[jax.ShapeDtypeStruct(below.shape, jnp.float32)] * size,
        in_specs=[VMEM] * (size + 1),
        out_specs=[VMEM] * size,
        compiler_params=pltpu.CompilerParams(vmem_limit_bytes=16 * 2**20),
        name="halo",
    )(*blocks, below)


def low_half(rows=1):
    return lax.broadcasted_iota(jnp.int32, (rows, W), 1) < F


def prepare(scale, parts, r, g, a_ref, b_ref, own_from=0, partner_from=0):
    low = low_half()
    rows = a_ref.shape[2]
    w = parts[0][r, own_from:rows]
    turned = pltpu.roll(w, F, 1)
    a_ref[0, g, own_from:rows] = turned * scale
    a_ref[1, g, own_from:rows] = (w + turned) * scale
    at = 0
    for part in parts:
        n = part.shape[1]
        skip = max(partner_from - at, 0)
        w = part[r, skip:]
        turned = pltpu.roll(w, F, 1)
        b_ref[0, g, at + skip : at + n] = jnp.where(low, turned - w, -(w + turned))
        b_ref[1, g, at + skip : at + n] = jnp.where(low, w, turned)
        at += n
    here = b_ref[1, g, partner_from:at]
    there = b_ref[1, g, partner_from + HALF : at + HALF]
    b_ref[1, g, partner_from:at] = jnp.where(low, here, there)


def step(q, tiles, row0, records, a_ref, b_ref, acc_ref, out_ref):
    low = low_half(SUB)

    def add(total, term):
        return term if total is None else total + term

    for u in range(HALF):
        s = row0 + SUB * q + u
        places, sums = [], []
        for i in tiles:
            rows = pl.ds(pl.multiple_of(row0 + SUB * i, SUB), SUB)
            k = SUB * (q - i) + u
            cols = [pl.ds(pl.multiple_of(n * W, W), W) for n in (k, k + HALF)]
            places.append([(rows, col) for col in cols])
            sums.append([None] + [None if acc_ref is None else acc_ref[at] for at in places[-1]])
        for g in records:
            both = b_ref[1, g, pl.ds(s, SUB)]
            first = b_ref[0, g, pl.ds(s, SUB)]
            second = b_ref[0, g, pl.ds(s + HALF, SUB)]
            for x, i in enumerate(tiles):
                own = a_ref[0, g, pl.ds(pl.multiple_of(row0 + SUB * i, SUB), SUB)]
                whole = a_ref[1, g, pl.ds(pl.multiple_of(row0 + SUB * i, SUB), SUB)]
                p, t1, t2 = sums[x]
                sums[x] = [add(p, whole * both), add(t1, own * first), add(t2, own * second)]
        for (here, there), (p, t1, t2) in zip(places, sums):
            turned = pltpu.roll(p, F, 1)
            out_ref[here] = t1 + jnp.where(low, p, turned)
            out_ref[there] = t2 + jnp.where(low, turned, p)


def sweep(records, region, rows, a_ref, b_ref, acc_ref, out_ref):
    tiles = 8 if rows % (8 * SUB) == 0 else 4
    spans = rows // (SUB * tiles)
    last = STEPS + tiles - 1
    bound = rows // SUB - 1
    args = (records, a_ref, b_ref, acc_ref, out_ref)

    def run(q, some, row0):
        step(q, some, row0, *args)

    def span(c, carry):
        row0 = pl.multiple_of(c * (SUB * tiles), SUB * tiles)
        edge = bound - tiles * c
        lo, hi = tiles - 1, STEPS
        if region == "main":
            hi = jnp.clip(edge, tiles - 1, STEPS)
        if region == "halo":
            lo = jnp.clip(edge, tiles - 1, STEPS)
        if region != "halo":
            for q in range(tiles - 1):
                run(q, list(range(q + 1)), row0)
        lax.fori_loop(lo, hi, lambda q, n: (run(q, list(range(tiles)), row0), n)[1], 0)

        def tail():
            for q in range(STEPS, last):
                run(q, list(range(q - STEPS + 1, tiles)), row0)

        if region == "main":
            pl.when(edge >= last)(tail)
        else:
            tail()
        return carry

    first = spans - STEPS // tiles if region == "halo" else 0
    lax.fori_loop(first, spans, span, 0)


def cross_kernel(scale, counts, region, has_acc, rows, *refs):
    refs = list(refs)
    acc_ref = refs.pop(0) if has_acc else None
    groups = [[refs.pop(0) for _ in range(n)] for n in counts]
    out_ref, a_ref, b_ref = refs
    g = 0
    for parts in groups:
        for r in range(parts[0].shape[0]):
            prepare(scale, parts, r, g, a_ref, b_ref)
            g += 1
    sweep(range(g), region, rows, a_ref, b_ref, acc_ref, out_ref)


def slabs(rows, halo, source, out_hbm, sems):
    top = rows - K
    tiles = K // SUB
    places = [] if halo else [((0, top), (0, K))]
    for i in range(tiles):
        edge = K - SUB * (i + 1)
        lo, hi = (edge, K) if halo else (0, edge)
        if hi > lo:
            places.append(((top + SUB * i, SUB), (lo, hi - lo)))
    copies = []
    for (row, n), (col, m) in places:
        at = (pl.ds(row, n), pl.ds(col * W, m * W))
        copies.append(pltpu.make_async_copy(source.at[at], out_hbm.at[at], sems.at[len(copies)]))
    return copies


def halo_sums(scale, groups, a_ref, b_ref, acc_ref, out_ref):
    rows = a_ref.shape[2]
    g = 0
    for parts in groups:
        for r in range(parts[0].shape[0]):
            prepare(scale, parts, r, g, a_ref, b_ref, rows - K, rows - 2 * SUB)
            g += 1
    sweep(range(g), "halo", rows, a_ref, b_ref, acc_ref, out_ref)


def edge_kernel(scale, count, rows, acc_ref, *refs):
    groups = [refs[2 * i : 2 * i + 2] for i in range(count)]
    out_hbm, tail_ref, a_ref, b_ref, sems = refs[2 * count :]
    copies = slabs(rows, False, acc_ref, out_hbm, sems)
    for copy in copies:
        copy.start()
    halo_sums(scale, groups, a_ref, b_ref, None, tail_ref)
    for copy in copies:
        copy.wait()


def finish_kernel(scale, rows, part_hbm, tail_ref, main_ref, halo_ref, out_hbm, sum_ref, a_ref, b_ref, sems):
    halo_sums(scale, [[main_ref, halo_ref]], a_ref, b_ref, tail_ref, sum_ref)
    copies = slabs(rows, True, sum_ref, out_hbm, sems)
    for copy in copies:
        copy.start()
    for copy in copies:
        copy.wait()


def cost(records, rows):
    return pl.CostEstimate(flops=500 * records * rows * K * W, bytes_accessed=0, transcendentals=0)


def factors(records, rows):
    return [
        pltpu.VMEM((2, records, rows, W), jnp.float32),
        pltpu.VMEM((2, records, rows + K + SUB, W), jnp.float32),
    ]


PARAMS = pltpu.CompilerParams(vmem_limit_bytes=24 * 2**20)


def cross(groups, region, rows, scale, acc=None):
    records = sum(g[0].shape[0] for g in groups)
    flat = [p for g in groups for p in g]
    return pl.pallas_call(
        functools.partial(
            cross_kernel, scale, [len(g) for g in groups], region, acc is not None, rows
        ),
        out_shape=jax.ShapeDtypeStruct((rows, K * W), jnp.float32),
        in_specs=[VMEM] * (len(flat) + (acc is not None)),
        out_specs=VMEM,
        scratch_shapes=factors(records, rows),
        input_output_aliases={0: 0} if acc is not None else {},
        compiler_params=PARAMS,
        cost_estimate=cost(records, rows),
        name="cross",
    )(*([acc] if acc is not None else []), *flat)


def edge(acc, groups, rows, scale):
    records = sum(g[0].shape[0] for g in groups)
    flat = [p for g in groups for p in g]
    out = jax.ShapeDtypeStruct((rows, K * W), jnp.float32)
    return pl.pallas_call(
        functools.partial(edge_kernel, scale, len(groups), rows),
        out_shape=[out, out],
        in_specs=[VMEM] * (1 + len(flat)),
        out_specs=[HBM, VMEM],
        scratch_shapes=factors(records, rows) + [pltpu.SemaphoreType.DMA((K // SUB,))],
        compiler_params=PARAMS,
        cost_estimate=cost(records // 3, rows),
        name="edge",
    )(acc, *flat)


def finish(part, tail, main, halo, scale):
    records, rows, _ = main.shape
    return pl.pallas_call(
        functools.partial(finish_kernel, scale, rows),
        out_shape=jax.ShapeDtypeStruct((rows, K * W), jnp.float32),
        in_specs=[HBM] + [VMEM] * 3,
        out_specs=HBM,
        scratch_shapes=[pltpu.VMEM((rows, K * W), jnp.float32)]
        + factors(records, rows)
        + [pltpu.SemaphoreType.DMA((K // SUB,))],
        input_output_aliases={0: 0},
        compiler_params=PARAMS,
        cost_estimate=cost(records // 3, rows),
        name="finish",
    )(part, tail, main, halo)


def send(shard, by):
    size = lax.axis_size("rec")
    return lax.ppermute(shard, "rec", [(i, i ^ by) for i in range(size)])


def shifted(shard, axis, by):
    length = lax.axis_size(axis)
    pairs = [(i, i + by) for i in range(length) if 0 <= i + by < length]
    return lax.ppermute(shard, axis, pairs)


def per_device(strain):
    records, channels, _ = strain.shape
    size = lax.axis_size("rec")
    rows = channels // size
    scale = 1.0 / (records * size)
    if size == 4 and rows == 2 * K and records <= HALF:
        return four(strain, rows, scale)
    return general(strain, rows, scale)


def four(strain, rows, scale):
    pair = 2 if strain.shape[0] % 2 == 0 else 1

    def block(by):
        return (lambda me: lax.bitwise_xor(me, by) * rows, rows)

    far, one, two, own, head = whiten(strain, [block(3), block(1), block(2), block(0)], pair)
    below = shifted(head, "chan", -1)
    far_in, one_in, two_in = send(far, 3), send(one, 1), send(two, 2)
    own_halo, one_halo, two_halo, far_halo = halos([own, one, two, far], below)
    one_halo_in, two_halo_in, far_halo_in = send(one_halo, 1), send(two_halo, 2), send(far_halo, 3)
    acc = cross([[own], [far_in]], "main", rows, scale)
    acc = cross([[one_in], [two_in]], "main", rows, scale, acc)
    part, tail = edge(
        acc, [[own, own_halo], [one_in, one_halo_in], [two_in, two_halo_in]], rows, scale
    )
    return finish(part, tail, far_in, far_halo_in, scale)


def general(strain, rows, scale):
    records, channels, _ = strain.shape
    size = lax.axis_size("rec")
    me = lax.axis_index("rec")
    spectra, head = whiten(strain, [(lambda me: 0 * me, channels)], 1)
    below = shifted(head, "chan", -1)
    extended = jnp.concatenate([spectra, below], axis=1)
    acc = None
    for by in range(size):
        to = lax.rem(me + by, size)
        part = lax.dynamic_slice_in_dim(extended, to * rows, rows + K, 1)
        if by:
            part = lax.ppermute(part, "rec", [(i, (i + by) % size) for i in range(size)])
        for r in range(0, records, MOST):
            acc = cross([[part[r : r + MOST]]], "all", rows, scale, acc)
    return acc


def solution(mesh):
    placed = (P("rec", "chan", None),)
    return jax.shard_map(
        per_device, mesh=mesh, in_specs=placed, out_specs=P(("chan", "rec"), None), check_vma=False
    )
```

```python
import functools
import math

import jax
import jax.numpy as jnp
from jax import lax
from jax.experimental import pallas as pl
from jax.experimental.pallas import tpu as pltpu
from jax.sharding import PartitionSpec as P

S = 2048
F = 64
K = 64
BIN0 = 32
W = 2 * F
SUB = 8
STEPS = K // SUB
HALF = SUB // 2
MOST = 8
VMEM = pl.BlockSpec(memory_space=pltpu.VMEM)
HBM = pl.BlockSpec(memory_space=pltpu.HBM)


def fill_table(table_ref):
    fine = 64

    def angle(rows, every, turn):
        n = lax.broadcasted_iota(jnp.int32, (rows, W), 0) * every
        lane = lax.broadcasted_iota(jnp.int32, (rows, W), 1)
        phase = n * (BIN0 + lax.rem(lane, F)) + jnp.where(lane < F, 0, S // 4) * (every == 1) + turn
        return jnp.cos(lax.rem(phase, S).astype(jnp.float32) * (2.0 * math.pi / S))

    cos_a, sin_a = angle(S // fine, fine, 0), angle(S // fine, fine, 3 * S // 4)
    cos_b, sin_b = angle(fine, 1, 0), angle(fine, 1, 3 * S // 4)
    for i in range(S // fine):
        rows = cos_a[i : i + 1] * cos_b - sin_a[i : i + 1] * sin_b
        table_ref[fine * i : fine * (i + 1)] = rows.astype(jnp.bfloat16)


def whiten_kernel(jobs, pair, strain_hbm, *refs):
    outs, head_ref, refs = refs[: len(jobs)], refs[len(jobs)], refs[len(jobs) + 1 :]
    table_ref, sems, bufs = refs[0], refs[1], refs[2:]
    me = lax.axis_index("rec")
    copies = []
    for (start, rows), buf in zip(jobs, bufs):
        at = pl.multiple_of(start(me), rows)
        for r in range(0, buf.shape[0], pair):
            copy = pltpu.make_async_copy(
                strain_hbm.at[pl.ds(r, pair), pl.ds(at, rows), :],
                buf.at[pl.ds(r, pair)],
                sems.at[len(copies)],
            )
            copy.start()
            copies.append(copy)
    fill_table(table_ref)
    at = 0
    for (start, rows), buf, out in zip(jobs, bufs, outs):
        for r in range(0, buf.shape[0], pair):
            copies[at].wait()
            at += 1
            block = buf[r : r + pair].reshape(pair * rows, S)
            spec = jnp.dot(block, table_ref[...], preferred_element_type=jnp.float32)
            power = jnp.sum(spec * spec, axis=-1, keepdims=True) * (1.0 / F)
            out[r : r + pair] = (spec * lax.rsqrt(power + 1e-06)).reshape(pair, rows, W)

        @pl.when(start(me) == 0)
        def _():
            head_ref[...] = out[:, :K]


def whiten(strain, jobs, pair):
    records = strain.shape[0]
    total = sum(rows for _, rows in jobs)
    outs = [jax.ShapeDtypeStruct((records, rows, W), jnp.float32) for _, rows in jobs]
    outs.append(jax.ShapeDtypeStruct((records, K, W), jnp.float32))
    return pl.pallas_call(
        functools.partial(whiten_kernel, jobs, pair),
        out_shape=outs,
        in_specs=[HBM],
        out_specs=[VMEM] * len(outs),
        scratch_shapes=[
            pltpu.VMEM((S, W), jnp.bfloat16),
            pltpu.SemaphoreType.DMA((len(jobs) * (records // pair),)),
        ]
        + [pltpu.VMEM((records, rows, S), jnp.bfloat16) for _, rows in jobs],
        compiler_params=pltpu.CompilerParams(vmem_limit_bytes=50 * 2**20),
        cost_estimate=pl.CostEstimate(
            flops=2 * records * total * S * W,
            bytes_accessed=2 * records * total * S,
            transcendentals=0,
        ),
        name="whiten",
    )(strain)


def halo_kernel(size, *refs):
    blocks, below_ref, outs = refs[:size], refs[size], refs[size + 1 :]
    me = lax.axis_index("rec")
    for by, out in enumerate(outs):
        target = lax.bitwise_xor(me, by)
        for other in range(size):
            if other != by:

                @pl.when((target < size - 1) & (lax.bitwise_xor(me, other) == target + 1))
                def _():
                    out[...] = blocks[other][:, :K]

        @pl.when(target == size - 1)
        def _():
            out[...] = below_ref[...]


def halos(blocks, below):
    size = len(blocks)
    return pl.pallas_call(
        functools.partial(halo_kernel, size),
        out_shape=[jax.ShapeDtypeStruct(below.shape, jnp.float32)] * size,
        in_specs=[VMEM] * (size + 1),
        out_specs=[VMEM] * size,
        compiler_params=pltpu.CompilerParams(vmem_limit_bytes=16 * 2**20),
        name="halo",
    )(*blocks, below)


def low_half(rows=1):
    return lax.broadcasted_iota(jnp.int32, (rows, W), 1) < F


def prepare(scale, parts, r, g, a_ref, b_ref, own_from=0, partner_from=0):
    low = low_half()
    rows = a_ref.shape[2]
    w = parts[0][r, own_from:rows]
    turned = pltpu.roll(w, F, 1)
    a_ref[0, g, own_from:rows] = turned * scale
    a_ref[1, g, own_from:rows] = (w + turned) * scale
    at = 0
    for part in parts:
        n = part.shape[1]
        skip = max(partner_from - at, 0)
        w = part[r, skip:]
        turned = pltpu.roll(w, F, 1)
        b_ref[0, g, at + skip : at + n] = jnp.where(low, turned - w, -(w + turned))
        b_ref[1, g, at + skip : at + n] = jnp.where(low, w, turned)
        at += n
    here = b_ref[1, g, partner_from:at]
    there = b_ref[1, g, partner_from + HALF : at + HALF]
    b_ref[1, g, partner_from:at] = jnp.where(low, here, there)


def step(q, tiles, row0, records, a_ref, b_ref, acc_ref, out_ref):
    low = low_half(SUB)

    def add(total, term):
        return term if total is None else total + term

    for u in range(HALF):
        s = row0 + SUB * q + u
        places, sums = [], []
        for i in tiles:
            rows = pl.ds(pl.multiple_of(row0 + SUB * i, SUB), SUB)
            k = SUB * (q - i) + u
            cols = [pl.ds(pl.multiple_of(n * W, W), W) for n in (k, k + HALF)]
            places.append([(rows, col) for col in cols])
            sums.append([None] + [None if acc_ref is None else acc_ref[at] for at in places[-1]])
        for g in records:
            both = b_ref[1, g, pl.ds(s, SUB)]
            first = b_ref[0, g, pl.ds(s, SUB)]
            second = b_ref[0, g, pl.ds(s + HALF, SUB)]
            for x, i in enumerate(tiles):
                own = a_ref[0, g, pl.ds(pl.multiple_of(row0 + SUB * i, SUB), SUB)]
                whole = a_ref[1, g, pl.ds(pl.multiple_of(row0 + SUB * i, SUB), SUB)]
                p, t1, t2 = sums[x]
                sums[x] = [add(p, whole * both), add(t1, own * first), add(t2, own * second)]
        for (here, there), (p, t1, t2) in zip(places, sums):
            turned = pltpu.roll(p, F, 1)
            out_ref[here] = t1 + jnp.where(low, p, turned)
            out_ref[there] = t2 + jnp.where(low, turned, p)


def sweep(records, region, rows, a_ref, b_ref, acc_ref, out_ref):
    tiles = 8 if rows % (8 * SUB) == 0 else 4
    spans = rows // (SUB * tiles)
    last = STEPS + tiles - 1
    bound = rows // SUB - 1
    args = (records, a_ref, b_ref, acc_ref, out_ref)

    def run(q, some, row0):
        step(q, some, row0, *args)

    def span(c, carry):
        row0 = pl.multiple_of(c * (SUB * tiles), SUB * tiles)
        edge = bound - tiles * c
        lo, hi = tiles - 1, STEPS
        if region == "main":
            hi = jnp.clip(edge, tiles - 1, STEPS)
        if region == "halo":
            lo = jnp.clip(edge, tiles - 1, STEPS)
        if region != "halo":
            for q in range(tiles - 1):
                run(q, list(range(q + 1)), row0)
        lax.fori_loop(lo, hi, lambda q, n: (run(q, list(range(tiles)), row0), n)[1], 0)

        def tail():
            for q in range(STEPS, last):
                run(q, list(range(q - STEPS + 1, tiles)), row0)

        if region == "main":
            pl.when(edge >= last)(tail)
        else:
            tail()
        return carry

    first = spans - STEPS // tiles if region == "halo" else 0
    lax.fori_loop(first, spans, span, 0)


def cross_kernel(scale, counts, region, has_acc, rows, *refs):
    refs = list(refs)
    acc_ref = refs.pop(0) if has_acc else None
    groups = [[refs.pop(0) for _ in range(n)] for n in counts]
    out_ref, a_ref, b_ref = refs
    g = 0
    for parts in groups:
        for r in range(parts[0].shape[0]):
            prepare(scale, parts, r, g, a_ref, b_ref)
            g += 1
    sweep(range(g), region, rows, a_ref, b_ref, acc_ref, out_ref)


def slabs(rows, which, source, out_hbm, sems):
    top = rows - K
    if which == "top":
        places = [((0, top), (0, K))]
    else:
        places = []
        for i in range(K // SUB):
            edge = K - SUB * (i + 1)
            lo, hi = (edge, K) if which == "halo" else (0, edge)
            if hi > lo:
                places.append(((top + SUB * i, SUB), (lo, hi - lo)))
    copies = []
    for (row, n), (col, m) in places:
        at = (pl.ds(row, n), pl.ds(col * W, m * W))
        copies.append(pltpu.make_async_copy(source.at[at], out_hbm.at[at], sems.at[len(copies)]))
    return copies


def halo_factors(scale, groups, a_ref, b_ref):
    rows = a_ref.shape[2]
    g = 0
    for parts in groups:
        for r in range(parts[0].shape[0]):
            prepare(scale, parts, r, g, a_ref, b_ref, rows - K, rows - 2 * SUB)
            g += 1
    return range(g)


def edge_kernel(scale, count, rows, acc_ref, *refs):
    groups = [refs[2 * i : 2 * i + 2] for i in range(count)]
    out_hbm, tail_ref, a_ref, b_ref, sems = refs[2 * count :]
    copies = slabs(rows, "top", acc_ref, out_hbm, sems)
    for copy in copies:
        copy.start()
    records = halo_factors(scale, groups, a_ref, b_ref)
    for i in range(STEPS):
        step(STEPS - 1 + i, list(range(i, STEPS)), rows - K, records, a_ref, b_ref, None, tail_ref)
    for copy in copies:
        copy.wait()


def finish_kernel(scale, count, rows, part_hbm, acc_ref, tail_ref, *refs):
    groups = [refs[2 * i : 2 * i + 2] for i in range(count)]
    out_hbm, sum_ref, a_ref, b_ref, sems = refs[2 * count :]
    early = slabs(rows, "main", acc_ref, out_hbm, sems.at[0])
    for copy in early:
        copy.start()
    records = halo_factors(scale, groups, a_ref, b_ref)
    late = slabs(rows, "halo", sum_ref, out_hbm, sems.at[1])
    for i, copy in enumerate(late):
        step(STEPS - 1 + i, list(range(i, STEPS)), rows - K, records, a_ref, b_ref, tail_ref, sum_ref)
        copy.start()
    for copy in early + late:
        copy.wait()


def cost(records, rows):
    return pl.CostEstimate(flops=500 * records * rows * K * W, bytes_accessed=0, transcendentals=0)


def factors(records, rows):
    return [
        pltpu.VMEM((2, records, rows, W), jnp.float32),
        pltpu.VMEM((2, records, rows + K + SUB, W), jnp.float32),
    ]


PARAMS = pltpu.CompilerParams(vmem_limit_bytes=24 * 2**20)


def cross(groups, region, rows, scale, acc=None):
    records = sum(g[0].shape[0] for g in groups)
    flat = [p for g in groups for p in g]
    return pl.pallas_call(
        functools.partial(
            cross_kernel, scale, [len(g) for g in groups], region, acc is not None, rows
        ),
        out_shape=jax.ShapeDtypeStruct((rows, K * W), jnp.float32),
        in_specs=[VMEM] * (len(flat) + (acc is not None)),
        out_specs=VMEM,
        scratch_shapes=factors(records, rows),
        compiler_params=PARAMS,
        cost_estimate=cost(records, rows),
        name="cross",
    )(*([acc] if acc is not None else []), *flat)


def edge(acc, groups, rows, scale):
    records = sum(g[0].shape[0] for g in groups)
    flat = [p for g in groups for p in g]
    out = jax.ShapeDtypeStruct((rows, K * W), jnp.float32)
    return pl.pallas_call(
        functools.partial(edge_kernel, scale, len(groups), rows),
        out_shape=[out, out],
        in_specs=[VMEM] * (1 + len(flat)),
        out_specs=[HBM, VMEM],
        scratch_shapes=factors(records, rows) + [pltpu.SemaphoreType.DMA((1,))],
        compiler_params=PARAMS,
        cost_estimate=cost(records // 2, rows),
        name="edge",
    )(acc, *flat)


def finish(part, acc, tail, groups, rows, scale):
    records = sum(g[0].shape[0] for g in groups)
    flat = [p for g in groups for p in g]
    return pl.pallas_call(
        functools.partial(finish_kernel, scale, len(groups), rows),
        out_shape=jax.ShapeDtypeStruct((rows, K * W), jnp.float32),
        in_specs=[HBM] + [VMEM] * (2 + len(flat)),
        out_specs=HBM,
        scratch_shapes=[pltpu.VMEM((rows, K * W), jnp.float32)]
        + factors(records, rows)
        + [pltpu.SemaphoreType.DMA((2, K // SUB))],
        input_output_aliases={0: 0},
        compiler_params=PARAMS,
        cost_estimate=cost(records // 2, rows),
        name="finish",
    )(part, acc, tail, *flat)


def send(shard, by):
    size = lax.axis_size("rec")
    return lax.ppermute(shard, "rec", [(i, i ^ by) for i in range(size)])


def shifted(shard, axis, by):
    length = lax.axis_size(axis)
    pairs = [(i, i + by) for i in range(length) if 0 <= i + by < length]
    return lax.ppermute(shard, axis, pairs)


def per_device(strain):
    records, channels, _ = strain.shape
    size = lax.axis_size("rec")
    rows = channels // size
    scale = 1.0 / (records * size)
    if size == 4 and rows == 2 * K and records <= HALF:
        return four(strain, rows, scale)
    return general(strain, rows, scale)


def four(strain, rows, scale):
    pair = 2 if strain.shape[0] % 2 == 0 else 1

    def block(by):
        return (lambda me: lax.bitwise_xor(me, by) * rows, rows)

    one, two, head_a = whiten(strain, [block(1), block(2)], pair)
    one_in, two_in = send(one, 1), send(two, 2)
    far, own, head_b = whiten(strain, [block(3), block(0)], pair)
    far_in = send(far, 3)
    me = lax.axis_index("rec")
    head = jnp.where((me == 1) | (me == 2), head_a, head_b)
    below = shifted(head, "chan", -1)
    own_halo, one_halo, two_halo, far_halo = halos([own, one, two, far], below)
    one_halo_in, two_halo_in, far_halo_in = send(one_halo, 1), send(two_halo, 2), send(far_halo, 3)
    acc = cross([[own]], "main", rows, scale)
    acc = cross([[one_in], [two_in], [far_in]], "main", rows, scale, acc)
    part, tail = edge(acc, [[own, own_halo], [one_in, one_halo_in]], rows, scale)
    return finish(part, acc, tail, [[two_in, two_halo_in], [far_in, far_halo_in]], rows, scale)


def general(strain, rows, scale):
    records, channels, _ = strain.shape
    size = lax.axis_size("rec")
    me = lax.axis_index("rec")
    spectra, head = whiten(strain, [(lambda me: 0 * me, channels)], 1)
    below = shifted(head, "chan", -1)
    extended = jnp.concatenate([spectra, below], axis=1)
    acc = None
    for by in range(size):
        to = lax.rem(me + by, size)
        part = lax.dynamic_slice_in_dim(extended, to * rows, rows + K, 1)
        if by:
            part = lax.ppermute(part, "rec", [(i, (i + by) % size) for i in range(size)])
        for r in range(0, records, MOST):
            acc = cross([[part[r : r + MOST]]], "all", rows, scale, acc)
    return acc


def solution(mesh):
    placed = (P("rec", "chan", None),)
    return jax.shard_map(
        per_device, mesh=mesh, in_specs=placed, out_specs=P(("chan", "rec"), None), check_vma=False
    )
```

```python
import functools
import math

import jax
import jax.numpy as jnp
from jax import lax
from jax.experimental import pallas as pl
from jax.experimental.pallas import tpu as pltpu
from jax.sharding import PartitionSpec as P

S = 2048
F = 64
K = 64
BIN0 = 32
W = 2 * F
SUB = 8
STEPS = K // SUB
HALF = SUB // 2
MOST = 8
VMEM = pl.BlockSpec(memory_space=pltpu.VMEM)
HBM = pl.BlockSpec(memory_space=pltpu.HBM)


def fill_table(table_ref):
    fine = 64

    def angle(rows, every, turn):
        n = lax.broadcasted_iota(jnp.int32, (rows, W), 0) * every
        lane = lax.broadcasted_iota(jnp.int32, (rows, W), 1)
        phase = n * (BIN0 + lax.rem(lane, F)) + jnp.where(lane < F, 0, S // 4) * (every == 1) + turn
        return jnp.cos(lax.rem(phase, S).astype(jnp.float32) * (2.0 * math.pi / S))

    cos_a, sin_a = angle(S // fine, fine, 0), angle(S // fine, fine, 3 * S // 4)
    cos_b, sin_b = angle(fine, 1, 0), angle(fine, 1, 3 * S // 4)
    for i in range(S // fine):
        rows = cos_a[i : i + 1] * cos_b - sin_a[i : i + 1] * sin_b
        table_ref[fine * i : fine * (i + 1)] = rows.astype(jnp.bfloat16)


def whiten_kernel(jobs, pair, strain_hbm, *refs):
    outs, refs = refs[: len(jobs)], refs[len(jobs) :]
    table_ref, sems, bufs = refs[0], refs[1], refs[2:]
    me = lax.axis_index("rec")
    copies = []
    for (start, rows), buf in zip(jobs, bufs):
        at = pl.multiple_of(start(me), rows)
        for r in range(0, buf.shape[0], pair):
            copy = pltpu.make_async_copy(
                strain_hbm.at[pl.ds(r, pair), pl.ds(at, rows), :],
                buf.at[pl.ds(r, pair)],
                sems.at[len(copies)],
            )
            copy.start()
            copies.append(copy)
    fill_table(table_ref)
    at = 0
    for (start, rows), buf, out in zip(jobs, bufs, outs):
        for r in range(0, buf.shape[0], pair):
            copies[at].wait()
            at += 1
            block = buf[r : r + pair].reshape(pair * rows, S)
            spec = jnp.dot(block, table_ref[...], preferred_element_type=jnp.float32)
            power = jnp.sum(spec * spec, axis=-1, keepdims=True) * (1.0 / F)
            out[r : r + pair] = (spec * lax.rsqrt(power + 1e-06)).reshape(pair, rows, W)


def whiten(strain, jobs, pair):
    records = strain.shape[0]
    total = sum(rows for _, rows in jobs)
    outs = [jax.ShapeDtypeStruct((records, rows, W), jnp.float32) for _, rows in jobs]
    return pl.pallas_call(
        functools.partial(whiten_kernel, jobs, pair),
        out_shape=outs,
        in_specs=[HBM],
        out_specs=[VMEM] * len(outs),
        scratch_shapes=[
            pltpu.VMEM((S, W), jnp.bfloat16),
            pltpu.SemaphoreType.DMA((len(jobs) * (records // pair),)),
        ]
        + [pltpu.VMEM((records, rows, S), jnp.bfloat16) for _, rows in jobs],
        compiler_params=pltpu.CompilerParams(vmem_limit_bytes=50 * 2**20),
        cost_estimate=pl.CostEstimate(
            flops=2 * records * total * S * W,
            bytes_accessed=2 * records * total * S,
            transcendentals=0,
        ),
        name="whiten",
    )(strain)


def halo_kernel(size, *refs):
    blocks, below_ref, outs = refs[:size], refs[size], refs[size + 1 :]
    me = lax.axis_index("rec")
    for by, out in enumerate(outs):
        target = lax.bitwise_xor(me, by)
        for other in range(size):
            if other != by:

                @pl.when((target < size - 1) & (lax.bitwise_xor(me, other) == target + 1))
                def _():
                    out[...] = blocks[other][:, :K]

        @pl.when(target == size - 1)
        def _():
            out[...] = below_ref[...]


def halos(blocks, below):
    size = len(blocks)
    return pl.pallas_call(
        functools.partial(halo_kernel, size),
        out_shape=[jax.ShapeDtypeStruct(below.shape, jnp.float32)] * size,
        in_specs=[VMEM] * (size + 1),
        out_specs=[VMEM] * size,
        compiler_params=pltpu.CompilerParams(vmem_limit_bytes=16 * 2**20),
        name="halo",
    )(*blocks, below)


def low_half(rows=1):
    return lax.broadcasted_iota(jnp.int32, (rows, W), 1) < F


def prepare(scale, parts, r, g, a_ref, b_ref, own_from=0, partner_from=0):
    low = low_half()
    rows = a_ref.shape[2]
    w = parts[0][r, own_from:rows]
    turned = pltpu.roll(w, F, 1)
    a_ref[0, g, own_from:rows] = turned * scale
    a_ref[1, g, own_from:rows] = (w + turned) * scale
    at = 0
    for part in parts:
        n = part.shape[1]
        skip = max(partner_from - at, 0)
        w = part[r, skip:]
        turned = pltpu.roll(w, F, 1)
        b_ref[0, g, at + skip : at + n] = jnp.where(low, turned - w, -(w + turned))
        b_ref[1, g, at + skip : at + n] = jnp.where(low, w, turned)
        at += n
    here = b_ref[1, g, partner_from:at]
    there = b_ref[1, g, partner_from + HALF : at + HALF]
    b_ref[1, g, partner_from:at] = jnp.where(low, here, there)


def step(q, tiles, row0, records, a_ref, b_ref, acc_ref, out_ref):
    low = low_half(SUB)

    def add(total, term):
        return term if total is None else total + term

    for u in range(HALF):
        s = row0 + SUB * q + u
        places, sums = [], []
        for i in tiles:
            rows = pl.ds(pl.multiple_of(row0 + SUB * i, SUB), SUB)
            k = SUB * (q - i) + u
            cols = [pl.ds(pl.multiple_of(n * W, W), W) for n in (k, k + HALF)]
            places.append([(rows, col) for col in cols])
            sums.append([None] + [None if acc_ref is None else acc_ref[at] for at in places[-1]])
        for g in records:
            both = b_ref[1, g, pl.ds(s, SUB)]
            first = b_ref[0, g, pl.ds(s, SUB)]
            second = b_ref[0, g, pl.ds(s + HALF, SUB)]
            for x, i in enumerate(tiles):
                own = a_ref[0, g, pl.ds(pl.multiple_of(row0 + SUB * i, SUB), SUB)]
                whole = a_ref[1, g, pl.ds(pl.multiple_of(row0 + SUB * i, SUB), SUB)]
                p, t1, t2 = sums[x]
                sums[x] = [add(p, whole * both), add(t1, own * first), add(t2, own * second)]
        for (here, there), (p, t1, t2) in zip(places, sums):
            turned = pltpu.roll(p, F, 1)
            out_ref[here] = t1 + jnp.where(low, p, turned)
            out_ref[there] = t2 + jnp.where(low, turned, p)


def sweep(records, region, rows, a_ref, b_ref, acc_ref, out_ref):
    tiles = 8 if rows % (8 * SUB) == 0 else 4
    spans = rows // (SUB * tiles)
    last = STEPS + tiles - 1
    bound = rows // SUB - 1
    args = (records, a_ref, b_ref, acc_ref, out_ref)

    def run(q, some, row0):
        step(q, some, row0, *args)

    def span(c, carry):
        row0 = pl.multiple_of(c * (SUB * tiles), SUB * tiles)
        edge = bound - tiles * c
        lo, hi = tiles - 1, STEPS
        if region == "main":
            hi = jnp.clip(edge, tiles - 1, STEPS)
        if region == "halo":
            lo = jnp.clip(edge, tiles - 1, STEPS)
        if region != "halo":
            for q in range(tiles - 1):
                run(q, list(range(q + 1)), row0)
        lax.fori_loop(lo, hi, lambda q, n: (run(q, list(range(tiles)), row0), n)[1], 0)

        def tail():
            for q in range(STEPS, last):
                run(q, list(range(q - STEPS + 1, tiles)), row0)

        if region == "main":
            pl.when(edge >= last)(tail)
        else:
            tail()
        return carry

    first = spans - STEPS // tiles if region == "halo" else 0
    lax.fori_loop(first, spans, span, 0)


def cross_kernel(scale, counts, region, has_acc, rows, *refs):
    refs = list(refs)
    acc_ref = refs.pop(0) if has_acc else None
    groups = [[refs.pop(0) for _ in range(n)] for n in counts]
    out_ref, a_ref, b_ref = refs
    g = 0
    for parts in groups:
        for r in range(parts[0].shape[0]):
            prepare(scale, parts, r, g, a_ref, b_ref)
            g += 1
    sweep(range(g), region, rows, a_ref, b_ref, acc_ref, out_ref)


def slabs(rows, which, source, out_hbm, sems):
    top = rows - K
    if which == "top":
        places = [((0, top), (0, K))]
    else:
        places = []
        for i in range(K // SUB):
            edge = K - SUB * (i + 1)
            lo, hi = (edge, K) if which == "halo" else (0, edge)
            if hi > lo:
                places.append(((top + SUB * i, SUB), (lo, hi - lo)))
    copies = []
    for (row, n), (col, m) in places:
        at = (pl.ds(row, n), pl.ds(col * W, m * W))
        copies.append(pltpu.make_async_copy(source.at[at], out_hbm.at[at], sems.at[len(copies)]))
    return copies


def halo_factors(scale, groups, a_ref, b_ref):
    rows = a_ref.shape[2]
    g = 0
    for parts in groups:
        for r in range(parts[0].shape[0]):
            prepare(scale, parts, r, g, a_ref, b_ref, rows - K, rows - 2 * SUB)
            g += 1
    return range(g)


def edge_kernel(scale, count, rows, acc_ref, *refs):
    groups = [refs[2 * i : 2 * i + 2] for i in range(count)]
    out_hbm, tail_ref, a_ref, b_ref, sems = refs[2 * count :]
    copies = slabs(rows, "top", acc_ref, out_hbm, sems)
    for copy in copies:
        copy.start()
    records = halo_factors(scale, groups, a_ref, b_ref)
    for i in range(STEPS):
        step(STEPS - 1 + i, list(range(i, STEPS)), rows - K, records, a_ref, b_ref, None, tail_ref)
    for copy in copies:
        copy.wait()


def finish_kernel(scale, count, rows, part_hbm, acc_ref, tail_ref, *refs):
    groups = [refs[2 * i : 2 * i + 2] for i in range(count)]
    out_hbm, sum_ref, a_ref, b_ref, sems = refs[2 * count :]
    early = slabs(rows, "main", acc_ref, out_hbm, sems.at[0])
    for copy in early:
        copy.start()
    records = halo_factors(scale, groups, a_ref, b_ref)
    late = slabs(rows, "halo", sum_ref, out_hbm, sems.at[1])
    for i, copy in enumerate(late):
        step(STEPS - 1 + i, list(range(i, STEPS)), rows - K, records, a_ref, b_ref, tail_ref, sum_ref)
        copy.start()
    for copy in early + late:
        copy.wait()


def cost(records, rows):
    return pl.CostEstimate(flops=500 * records * rows * K * W, bytes_accessed=0, transcendentals=0)


def factors(records, rows):
    return [
        pltpu.VMEM((2, records, rows, W), jnp.float32),
        pltpu.VMEM((2, records, rows + K + SUB, W), jnp.float32),
    ]


PARAMS = pltpu.CompilerParams(vmem_limit_bytes=24 * 2**20)


def cross(groups, region, rows, scale, acc=None):
    records = sum(g[0].shape[0] for g in groups)
    flat = [p for g in groups for p in g]
    return pl.pallas_call(
        functools.partial(
            cross_kernel, scale, [len(g) for g in groups], region, acc is not None, rows
        ),
        out_shape=jax.ShapeDtypeStruct((rows, K * W), jnp.float32),
        in_specs=[VMEM] * (len(flat) + (acc is not None)),
        out_specs=VMEM,
        scratch_shapes=factors(records, rows),
        compiler_params=PARAMS,
        cost_estimate=cost(records, rows),
        name="cross",
    )(*([acc] if acc is not None else []), *flat)


def edge(acc, groups, rows, scale):
    records = sum(g[0].shape[0] for g in groups)
    flat = [p for g in groups for p in g]
    out = jax.ShapeDtypeStruct((rows, K * W), jnp.float32)
    return pl.pallas_call(
        functools.partial(edge_kernel, scale, len(groups), rows),
        out_shape=[out, out],
        in_specs=[VMEM] * (1 + len(flat)),
        out_specs=[HBM, VMEM],
        scratch_shapes=factors(records, rows) + [pltpu.SemaphoreType.DMA((1,))],
        compiler_params=PARAMS,
        cost_estimate=cost(records // 2, rows),
        name="edge",
    )(acc, *flat)


def finish(part, acc, tail, groups, rows, scale):
    records = sum(g[0].shape[0] for g in groups)
    flat = [p for g in groups for p in g]
    return pl.pallas_call(
        functools.partial(finish_kernel, scale, len(groups), rows),
        out_shape=jax.ShapeDtypeStruct((rows, K * W), jnp.float32),
        in_specs=[HBM] + [VMEM] * (2 + len(flat)),
        out_specs=HBM,
        scratch_shapes=[pltpu.VMEM((rows, K * W), jnp.float32)]
        + factors(records, rows)
        + [pltpu.SemaphoreType.DMA((2, K // SUB))],
        input_output_aliases={0: 0},
        compiler_params=PARAMS,
        cost_estimate=cost(records // 2, rows),
        name="finish",
    )(part, acc, tail, *flat)


def send(shard, by):
    size = lax.axis_size("rec")
    return lax.ppermute(shard, "rec", [(i, i ^ by) for i in range(size)])


def shifted(shard, axis, by):
    length = lax.axis_size(axis)
    pairs = [(i, i + by) for i in range(length) if 0 <= i + by < length]
    return lax.ppermute(shard, axis, pairs)


def per_device(strain):
    records, channels, _ = strain.shape
    size = lax.axis_size("rec")
    rows = channels // size
    scale = 1.0 / (records * size)
    if size == 4 and rows == 2 * K and records <= HALF:
        return four(strain, rows, scale)
    return general(strain, rows, scale)


def four(strain, rows, scale):
    pair = 2 if strain.shape[0] % 2 == 0 else 1

    def block(by):
        return (lambda me: lax.bitwise_xor(me, by) * rows, rows)

    far, head = whiten(strain, [block(3), (lambda me: 0 * me, K)], pair)
    below = shifted(head, "chan", -1)
    far_in = send(far, 3)
    one, two = whiten(strain, [block(1), block(2)], pair)
    (own,) = whiten(strain, [block(0)], pair)
    one_in, two_in = send(one, 1), send(two, 2)
    own_halo, one_halo, two_halo, far_halo = halos([own, one, two, far], below)
    one_halo_in, two_halo_in, far_halo_in = send(one_halo, 1), send(two_halo, 2), send(far_halo, 3)
    acc = cross([[own], [far_in]], "main", rows, scale)
    acc = cross([[one_in], [two_in]], "main", rows, scale, acc)
    part, tail = edge(acc, [[own, own_halo], [one_in, one_halo_in]], rows, scale)
    return finish(part, acc, tail, [[two_in, two_halo_in], [far_in, far_halo_in]], rows, scale)


def general(strain, rows, scale):
    records, channels, _ = strain.shape
    size = lax.axis_size("rec")
    me = lax.axis_index("rec")
    (spectra,) = whiten(strain, [(lambda me: 0 * me, channels)], 1)
    below = shifted(spectra[:, :K], "chan", -1)
    extended = jnp.concatenate([spectra, below], axis=1)
    acc = None
    for by in range(size):
        to = lax.rem(me + by, size)
        part = lax.dynamic_slice_in_dim(extended, to * rows, rows + K, 1)
        if by:
            part = lax.ppermute(part, "rec", [(i, (i + by) % size) for i in range(size)])
        for r in range(0, records, MOST):
            acc = cross([[part[r : r + MOST]]], "all", rows, scale, acc)
    return acc


def solution(mesh):
    placed = (P("rec", "chan", None),)
    return jax.shard_map(
        per_device, mesh=mesh, in_specs=placed, out_specs=P(("chan", "rec"), None), check_vma=False
    )
```
